256 devices in a mesh: opg: 16 (over z, x_lo), sec: 16 (over x_hi, y, core).
Axes of the slice: x: 4 (x_hi: 2, x_lo: 2; x = x_hi * 2 + x_lo), y: 4, z: 8, core: 2. Of those that a mesh axis runs over, the one named last changes fastest.
Arguments:
- psi: bfloat16 [32, 384, 384], P('sec'), may hold values from -6 to 6
- left_ops: bfloat16 [128, 32, 384, 384], P('opg', 'sec'), may hold values from -0.15625 to 0.15625
- right_ops: bfloat16 [128, 32, 384, 384], P('opg', 'sec'), may hold values from -0.109375 to 0.109375
- source: int32 [128, 32], P('opg', 'sec'), may hold values from 0 to 31
- coef_index: int32 [128, 32], P('opg', 'sec'), may hold values from 0 to 63
- sixj: float32 [64], replicated, may hold values from -1 to 1
Outputs:
- sigma: bfloat16 [384, 32, 384], P('opg', 'sec')
The draws below stay inside these ranges and needn't reach their ends.
All inputs are finite; a program needn't handle non-finite values.
Results may differ from the reference program's by a relative error of at most 0.005.
Values may be sent and summed in bfloat16 or wider, within the bound.
A program may use at most 64 MiB of HBM per device.

```python
import jax
import jax.numpy as jnp
from jax import lax

SB = 384
P_DEV = 8
NJ = 64
NS = 32
PAIRS = 128


def with_ends(drawn, rng, smallest, largest):
    longest = drawn.shape.index(max(drawn.shape))
    spots = []
    for shift in (0, 1):
        where = [jax.random.randint(jax.random.fold_in(rng, axis), (), 0, length) for axis, length in enumerate(drawn.shape)]
        where[longest] = (where[longest] + shift) % drawn.shape[longest]
        spots.append(tuple(where))
    return drawn.at[spots[0]].set(smallest).at[spots[1]].set(largest)


def levels(rng, extent, shards, smallest, largest):
    def one(position, parts):
        draws = jax.random.uniform(jax.random.fold_in(jax.random.fold_in(rng, 6), position), (parts,), jnp.float32, smallest / len(shards), largest / len(shards))
        return jnp.repeat(jnp.exp(draws), extent[position] // parts).reshape((-1,) + (1,) * (len(extent) - position - 1))

    gain = one(*shards[0])
    for cut in shards[1:]:
        gain = gain * one(*cut)
    return gain


def normal_values(own_key, shape, deviation, limit, shards=(), dtype=jnp.bfloat16):
    loudness = levels(own_key, shape, shards, -0.22, 0.18) if shards else 1.0
    values = jax.random.normal(own_key, shape, jnp.float32) * deviation * loudness
    return jnp.minimum(jnp.maximum(values, -limit), limit).astype(dtype)


def setup_inputs(seed: int = 0) -> dict:
    streams_of = jax.random.split(jax.random.key(seed), 7)
    psi = normal_values(streams_of[0], (NS, SB, SB), 1.0, 6.0, ((0, 16),))
    left_ops = normal_values(streams_of[1], (PAIRS, NS, SB, SB), (SB * 4) ** -0.5, 0.15625, ((0, 16), (1, 16)))
    right_ops = normal_values(streams_of[2], (PAIRS, NS, SB, SB), (SB * P_DEV) ** -0.5, 0.109375, ((0, 16), (1, 16)))
    source = with_ends(jax.random.randint(streams_of[3], (PAIRS, NS), 0, NS), jax.random.fold_in(streams_of[3], 1), 0, NS - 1).astype(jnp.int32)
    coef_index = with_ends(jax.random.randint(streams_of[4], (PAIRS, NS), 0, NJ), jax.random.fold_in(streams_of[4], 1), 0, NJ - 1).astype(jnp.int32)
    sixj = jnp.clip(jax.random.uniform(streams_of[5], (NJ,), jnp.float32, -1.0, 1.0), -1.0, 1.0)
    return {"psi": psi, "left_ops": left_ops, "right_ops": right_ops, "source": source, "coef_index": coef_index, "sixj": sixj}


def reference(psi, left_ops, right_ops, source, coef_index, sixj):
    coef = sixj[coef_index]

    def one_sector(s):
        left = left_ops[:, s].astype(jnp.float32)
        right = right_ops[:, s].astype(jnp.float32)
        picked = psi[source[:, s]].astype(jnp.float32)
        half = jnp.einsum("pib,pbc->pic", left, picked).astype(jnp.bfloat16)
        half = lax.optimization_barrier(half).astype(jnp.float32)
        full = jnp.einsum("pic,pjc->pij", half, right)
        return jnp.sum(full * coef[:, s][:, None, None], axis=0)

    total = lax.map(one_sector, jnp.arange(NS))
    return jnp.transpose(total, (1, 0, 2)).astype(jnp.bfloat16)
```

```python
import functools

import jax
import jax.numpy as jnp
from jax import lax
from jax.experimental import pallas as pl
from jax.experimental.pallas import tpu as pltpu
from jax.sharding import PartitionSpec as P

MESH = pl.DeviceIdType.MESH
SB = 384
CW = 128
NCH = SB // CW
NP = 8
ROWS = 24


class Place:
    def __init__(self):
        o, s = lax.axis_index("opg"), lax.axis_index("sec")
        self.z, self.xl = o // 2, o % 2
        self.xh, self.y, self.c = s // 8, (s // 2) % 4, s % 2
        self.colour = (self.xl + self.xh + self.z) % 2

    def at(self, z=None, xl=None, xh=None, y=None, c=None):
        z = self.z if z is None else z
        xl = self.xl if xl is None else xl
        xh = self.xh if xh is None else xh
        y = self.y if y is None else y
        c = self.c if c is None else c
        return (z * 2 + xl, (xh * 4 + y) * 2 + c)

    def neighbour(self, name):
        if name == "y+":
            return self.at(y=(self.y + 1) % 4)
        if name == "y-":
            return self.at(y=(self.y + 3) % 4)
        if name == "xc":
            return self.at(xl=1 - self.xl, xh=1 - self.xh)
        if name == "xp":
            return self.at(xl=1 - self.xl)
        if name == "z+":
            return self.at(z=(self.z + 1) % 8)
        if name == "z-":
            return self.at(z=(self.z + 7) % 8)
        assert name == "c"
        return self.at(c=1 - self.c)


def kernel(
    psi, left, right, source, coef_index, sixj, out,
    g0, g1, g2, lv, rv, hv, acc, sa, ra, sb, rb,
    load_sem, send_sem, recv_sem, rs_send, rs_recv,
):
    here = Place()
    gs = (g0, g1, g2)
    group = here.xh * 4 + here.y
    own = group * 4 + here.c * 2
    groups = {
        "O": group,
        "Y1": here.xh * 4 + (here.y + 1) % 4,
        "Y2": here.xh * 4 + (here.y + 2) % 4,
        "Y3": here.xh * 4 + (here.y + 3) % 4,
        "X0": (1 - here.xh) * 4 + here.y,
        "X1": (1 - here.xh) * 4 + (here.y + 1) % 4,
        "X2": (1 - here.xh) * 4 + (here.y + 2) % 4,
        "X3": (1 - here.xh) * 4 + (here.y + 3) % 4,
    }

    loads = [
        pltpu.make_async_copy(
            psi.at[:, :, pl.ds(k * CW, CW)], gs[k].at[pl.ds(own, 2)], load_sem.at[k]
        )
        for k in range(NCH)
    ]
    load_left = pltpu.make_async_copy(left, lv, load_sem.at[NCH])
    load_right = pltpu.make_async_copy(right, rv, load_sem.at[NCH + 1])
    for load in loads:
        load.start()
    load_left.start()
    load_right.start()

    barrier = pltpu.get_barrier_semaphore()
    near = [here.neighbour(n) for n in ("y+", "y-", "xc", "xp", "z+", "z-", "c")]
    far = [here.at(z=(here.z + d) % 8) for d in (2, 3, 4, 5, 6)]
    for device in near + far:
        pl.semaphore_signal(barrier, inc=1, device_id=device, device_id_type=MESH)
    pl.semaphore_wait(barrier, len(near) + len(far))

    slots = {}

    def message(k, name, to, who, lo, hi, both=False):
        slot = slots.setdefault(name, len(slots))
        if both:
            ref = gs[k].at[pl.ds(groups[who] * 4 + here.c * 2, 2)]
        else:
            ref = gs[k].at[groups[who] * 4 + here.c * 2 + here.colour, pl.ds(lo, hi - lo)]
        return pltpu.make_async_remote_copy(
            src_ref=ref,
            dst_ref=ref,
            send_sem=send_sem.at[k],
            recv_sem=recv_sem.at[k, slot],
            device_id=here.neighbour(to),
            device_id_type=MESH,
        )

    def send(k, name, to, who, lo=0, hi=SB, both=False):
        message(k, name, to, who, lo, hi, both).start()

    def recv(k, name, to, who, lo=0, hi=SB, both=False):
        message(k, name, to, who, lo, hi, both).wait_recv()

    PART = 320
    SWAP = {"Y1": "xp", "Y3": "z+", "X0": "z-", "Y2": "xp", "X1": "z+", "X3": "z-"}

    def swap(k, who):
        if who == "X2":
            for i, to in enumerate(("xp", "z+", "z-")):
                send(k, f"swap{who}{i}", to, who, i * 128, i * 128 + 128)
        else:
            send(k, f"swap{who}", SWAP[who], who)

    def swapped(k, who):
        if who == "X2":
            for i, to in enumerate(("xp", "z+", "z-")):
                recv(k, f"swap{who}{i}", to, who, i * 128, i * 128 + 128)
        else:
            recv(k, f"swap{who}", SWAP[who], who)
        send(k, f"core{who}", "c", who, both=True)

    def own_start(k):
        loads[k].wait()
        send(k, "Y3", "y+", "O")
        send(k, "Y1", "y-", "O")
        send(k, "X0", "xc", "O")
        send(k, "coreO", "c", "O", both=True)

    def got_y1(k):
        recv(k, "Y1", "y-", "O")
        send(k, "Y2b", "y-", "Y1", 192, SB)
        send(k, "X1b", "xc", "Y1", PART, SB)
        swap(k, "Y1")

    def got_y3(k):
        recv(k, "Y3", "y+", "O")
        send(k, "Y2a", "y+", "Y3", 0, 192)
        send(k, "X3b", "xc", "Y3", PART, SB)
        swap(k, "Y3")

    def got_x0(k):
        recv(k, "X0", "xc", "O")
        send(k, "X1a", "y-", "X0", 0, PART)
        send(k, "X3a", "y+", "X0", 0, PART)
        swap(k, "X0")

    def got_y2(k):
        recv(k, "Y2a", "y+", "Y3", 0, 192)
        send(k, "X2a", "xc", "Y2", 0, 192)
        recv(k, "Y2b", "y-", "Y1", 192, SB)
        send(k, "X2b", "xc", "Y2", 192, SB)
        swap(k, "Y2")

    def got_x1(k):
        recv(k, "X1a", "y-", "X0", 0, PART)
        recv(k, "X1b", "xc", "Y1", PART, SB)
        swap(k, "X1")

    def got_x3(k):
        recv(k, "X3a", "y+", "X0", 0, PART)
        recv(k, "X3b", "xc", "Y3", PART, SB)
        swap(k, "X3")

    def got_x2(k):
        recv(k, "X2a", "xc", "Y2", 0, 192)
        recv(k, "X2b", "xc", "Y2", 192, SB)
        swap(k, "X2")

    ALL = ("Y1", "Y3", "X0", "Y2", "X1", "X3", "X2")

    def gathered(k):
        for who in ("O",) + ALL:
            recv(k, f"core{who}", "c", who, both=True)

    def first(k, p, s):
        block = gs[k][source[p, s]]
        coef = sixj[coef_index[p, s]]
        half = jnp.dot(lv[p, s], block, preferred_element_type=jnp.float32)
        hv[s, p] = (half * coef).astype(jnp.bfloat16)

    def second(k, s):
        a = jnp.concatenate([hv[s, p] for p in range(NP)], axis=1)
        b = jnp.concatenate([rv[p, s, :, k * CW : (k + 1) * CW] for p in range(NP)], axis=1)
        part = lax.dot_general(
            a, b, (((1,), (1,)), ((), ())), preferred_element_type=jnp.float32
        ).reshape(8, 2, ROWS, SB)
        if k == 0:
            acc[s] = part
        else:
            acc[s] += part

    comm = [
        [
            functools.partial(own_start, k),
            functools.partial(got_y1, k),
            functools.partial(got_y3, k),
            functools.partial(got_x0, k),
            functools.partial(got_y2, k),
            functools.partial(got_x1, k),
            functools.partial(got_x3, k),
        ]
        + [functools.partial(swapped, k, w) for w in ALL[:3]]
        + [functools.partial(got_x2, k)]
        + [functools.partial(swapped, k, w) for w in ALL[3:]]
        + [functools.partial(gathered, k)]
        for k in range(NCH)
    ]
    work = [
        [
            step
            for s in range(2)
            for step in [functools.partial(first, k, p, s) for p in range(NP)]
            + [functools.partial(second, k, s)]
        ]
        for k in range(NCH)
    ]

    for k in range(NCH):
        steps = list(comm[k])
        todo = list(work[k - 1]) if k else []
        if k == 1:
            load_left.wait()
            load_right.wait()
        n, m = len(steps), len(todo)
        done = 0
        for i, step in enumerate(steps):
            step()
            upto = m * (i + 1) // n
            for task in todo[done:upto]:
                task()
            done = upto
    for task in work[NCH - 1]:
        task()

    mine, theirs = here.xl, 1 - here.xl
    order = (4, 3, 5, 2, 6, 1, 7, 0)
    pair = []
    for i, d in enumerate(order):
        z = (here.z + d) % 8
        sa[i] = jnp.concatenate([acc[0, z, theirs], acc[1, z, theirs]], axis=0).astype(jnp.bfloat16)
        copy = pltpu.make_async_remote_copy(
            src_ref=sa.at[i],
            dst_ref=ra.at[i],
            send_sem=rs_send.at[0],
            recv_sem=rs_recv.at[i],
            device_id=here.neighbour("xp"),
            device_id_type=MESH,
        )
        copy.start()
        pair.append(copy)
    total = None
    cross = []
    for i, d in enumerate(order):
        z = (here.z + d) % 8
        pair[i].wait_recv()
        both = jnp.concatenate([acc[0, z, mine], acc[1, z, mine]], axis=0) + ra[i].astype(jnp.float32)
        if d == 0:
            total = both
            continue
        sb[i] = both.astype(jnp.bfloat16)
        copy = pltpu.make_async_remote_copy(
            src_ref=sb.at[i],
            dst_ref=rb.at[i],
            send_sem=rs_send.at[1],
            recv_sem=rs_recv.at[8 + i],
            device_id=here.at(z=z),
            device_id_type=MESH,
        )
        copy.start()
        cross.append(copy)
    for i, copy in enumerate(cross):
        copy.wait_recv()
        total = total + rb[i].astype(jnp.float32)
    out[...] = total.astype(jnp.bfloat16)

    for k in range(NCH):
        ref = gs[k].at[pl.ds(0, 30)]
        pltpu.make_async_copy(ref, ref, send_sem.at[k]).wait()
    pltpu.make_async_copy(sa, sa, rs_send.at[0]).wait()
    pltpu.make_async_copy(sb, sb, rs_send.at[1]).wait()


def on_device(psi, left_ops, right_ops, source, coef_index, sixj):
    anywhere = pl.BlockSpec(memory_space=pl.ANY)
    scalars = pl.BlockSpec(memory_space=pltpu.SMEM)
    bf16, f32 = jnp.bfloat16, jnp.float32
    mine = pl.pallas_call(
        kernel,
        name="sigma",
        out_shape=jax.ShapeDtypeStruct((2 * ROWS, SB), bf16),
        in_specs=[anywhere] * 3 + [scalars] * 3,
        out_specs=pl.BlockSpec(memory_space=pltpu.VMEM),
        scratch_shapes=[pltpu.VMEM((32, SB, CW), bf16)] * NCH
        + [
            pltpu.VMEM((NP, 2, SB, SB), bf16),
            pltpu.VMEM((NP, 2, SB, SB), bf16),
            pltpu.VMEM((2, NP, SB, CW), bf16),
            pltpu.VMEM((2, 8, 2, ROWS, SB), f32),
            pltpu.VMEM((8, 2 * ROWS, SB), bf16),
            pltpu.VMEM((8, 2 * ROWS, SB), bf16),
            pltpu.VMEM((7, 2 * ROWS, SB), bf16),
            pltpu.VMEM((7, 2 * ROWS, SB), bf16),
            pltpu.SemaphoreType.DMA((NCH + 2,)),
            pltpu.SemaphoreType.DMA((NCH,)),
            pltpu.SemaphoreType.DMA((NCH, 28)),
            pltpu.SemaphoreType.DMA((2,)),
            pltpu.SemaphoreType.DMA((15,)),
        ],
        compiler_params=pltpu.CompilerParams(
            collective_id=0, has_side_effects=True, vmem_limit_bytes=48 * 2**20
        ),
    )(psi, left_ops, right_ops, source, coef_index, sixj)
    return jnp.transpose(mine.reshape(2, ROWS, SB), (1, 0, 2))


def solution(mesh):
    placed = (
        P("sec", None, None),
        P("opg", "sec", None, None),
        P("opg", "sec", None, None),
        P("opg", "sec"),
        P("opg", "sec"),
        P(),
    )
    return jax.shard_map(
        on_device, mesh=mesh, in_specs=placed, out_specs=P("opg", "sec", None), check_vma=False
    )
```

```python
import functools

import jax
import jax.numpy as jnp
from jax import lax
from jax.experimental import pallas as pl
from jax.experimental.pallas import tpu as pltpu
from jax.sharding import PartitionSpec as P

MESH = pl.DeviceIdType.MESH
SB = 384
WIDTHS = (1, 2)
NCH = len(WIDTHS)
COLS = [slice(128 * sum(WIDTHS[:k]), 128 * sum(WIDTHS[: k + 1])) for k in range(NCH)]
NP = 8
ROWS = 24


YP, YM, XC, XP, ZP, ZM, CORE, XPC, ZPC, ZMC = LINKS = range(10)
OWN, Y1, Y2, Y3, X0, X1, X2, X3 = range(8)
READY, WORK = -1, -2
MINE, OTHER, BOTH = range(3)
MESSAGES = (
    (
        (YM, OWN, 0, 384, MINE, ()),
        (YP, OWN, 0, 384, MINE, ()),
        (XC, OWN, 0, 384, MINE, ()),
        (YP, Y3, 0, 192, MINE, (1,)),
        (YM, Y1, 192, 384, MINE, (0,)),
        (YM, X0, 0, 320, MINE, (2,)),
        (YP, X0, 0, 320, MINE, (2,)),
        (XC, Y1, 320, 384, MINE, (0,)),
        (XC, Y3, 320, 384, MINE, (1,)),
        (XC, Y2, 0, 192, MINE, (3,)),
        (XC, Y2, 192, 384, MINE, (4,)),
        (ZM, Y1, 0, 384, MINE, (0,)),
        (XP, Y3, 0, 384, MINE, (1,)),
        (ZP, X0, 0, 384, MINE, (2,)),
        (XP, Y2, 0, 128, MINE, (3,)),
        (ZP, Y2, 128, 256, MINE, (3, 4)),
        (ZM, Y2, 256, 384, MINE, (4,)),
        (XP, X1, 0, 128, MINE, (5,)),
        (ZP, X1, 128, 256, MINE, (5,)),
        (ZM, X1, 256, 384, MINE, (5, 7)),
        (XP, X3, 0, 128, MINE, (6,)),
        (ZP, X3, 128, 256, MINE, (6,)),
        (ZM, X3, 256, 384, MINE, (6, 8)),
        (XP, X2, 0, 128, MINE, (9,)),
        (ZP, X2, 128, 256, MINE, (9, 10)),
        (ZM, X2, 256, 384, MINE, (10,)),
        (CORE, OWN, 0, 384, BOTH, ()),
        (CORE, Y1, 0, 384, BOTH, (0, 11)),
        (CORE, Y3, 0, 384, BOTH, (1, 12)),
        (CORE, X0, 0, 384, BOTH, (2, 13)),
        (CORE, Y2, 0, 384, BOTH, (3, 4, 14, 15, 16)),
        (CORE, X1, 0, 384, BOTH, (5, 7, 17, 18, 19)),
        (CORE, X3, 0, 384, BOTH, (6, 8, 20, 21, 22)),
        (CORE, X2, 0, 384, BOTH, (9, 10, 23, 24, 25)),
    ),
    (
        (YM, OWN, 0, 192, MINE, ()),
        (YM, OWN, 192, 384, MINE, ()),
        (YP, OWN, 0, 192, MINE, ()),
        (YP, OWN, 192, 384, MINE, ()),
        (XC, OWN, 0, 192, MINE, ()),
        (XC, OWN, 192, 384, MINE, ()),
        (YP, Y3, 0, 192, MINE, (2,)),
        (YM, Y1, 192, 384, MINE, (1,)),
        (YM, X0, 0, 128, MINE, (4,)),
        (YM, X0, 128, 256, MINE, (4, 5)),
        (YP, X0, 0, 128, MINE, (4,)),
        (YP, X0, 128, 256, MINE, (4, 5)),
        (XC, Y1, 256, 384, MINE, (1,)),
        (XC, Y3, 256, 384, MINE, (3,)),
        (YM, X1, 0, 64, MINE, (8,)),
        (YP, X3, 320, 384, MINE, (13,)),
        (XC, Y2, 64, 192, MINE, (6,)),
        (XC, Y2, 192, 320, MINE, (7,)),
        (XP, Y1, 0, 128, MINE, (0,)),
        (XP, Y1, 128, 256, MINE, (0, 1)),
        (XP, Y1, 256, 384, MINE, (1,)),
        (ZM, Y3, 0, 192, MINE, (2,)),
        (ZM, Y3, 192, 384, MINE, (3,)),
        (ZP, X0, 0, 192, MINE, (4,)),
        (ZP, X0, 192, 384, MINE, (5,)),
        (ZM, Y2, 0, 192, MINE, (6,)),
        (ZM, Y2, 192, 384, MINE, (7,)),
        (ZP, X1, 0, 128, MINE, (8,)),
        (ZP, X1, 128, 256, MINE, (9,)),
        (ZP, X1, 256, 384, MINE, (12,)),
        (XP, X3, 0, 128, MINE, (10,)),
        (XP, X3, 128, 256, MINE, (11,)),
        (XP, X3, 256, 384, MINE, (13,)),
        (XP, X2, 0, 128, MINE, (14, 16)),
        (XPC, X2, 0, 128, MINE, (14, 16)),
        (ZP, X2, 128, 256, MINE, (16, 17)),
        (ZPC, X2, 128, 256, MINE, (16, 17)),
        (ZM, X2, 256, 384, MINE, (15, 17)),
        (ZMC, X2, 256, 384, MINE, (15, 17)),
        (CORE, OWN, 0, 384, BOTH, ()),
        (CORE, Y1, 0, 384, BOTH, (0, 1, 18, 19, 20)),
        (CORE, Y3, 0, 384, BOTH, (2, 3, 21, 22)),
        (CORE, X0, 0, 384, BOTH, (4, 5, 23, 24)),
        (CORE, Y2, 0, 384, BOTH, (6, 7, 25, 26)),
        (CORE, X1, 0, 384, BOTH, (8, 9, 12, 27, 28, 29)),
        (CORE, X3, 0, 384, MINE, (10, 11, 13)),
        (CORE, X3, 0, 384, OTHER, (30, 31, 32)),
        (CORE, X2, 0, 384, MINE, (14, 15, 16, 17)),
    ),
)
ORDER = (
    (0, 0), (0, 1), (1, 5), (0, 26), (1, 39), (1, 1), (1, 2), (0, 2), (1, 0), (1, 3), (1, 4),
    (0, 11), (0, 12), (1, 24), (0, 4), (0, 3), (0, 7), (0, 8), (1, 20), (1, 21), (0, 13), (1, 6),
    (0, 5), (1, 12), (1, 7), (1, 19), (1, 22), (1, 23), (0, 6), (1, 13), (0, 28), (0, 27), (1, 18),
    (0, 10), (0, 16), (0, 15), (1, 8), (1, 10), (0, 9), (0, 14), (1, 29), (0, 29), (0, 19), (0, 17),
    (1, 25), (1, 16), (1, 9), (1, 11), (0, 18), (1, 32), (1, 41), (1, 42), (1, 15), (1, 17),
    (0, 21), (0, 22), (1, 40), (0, 20), (0, 25), (0, 30), (0, 23), (0, 24), (1, 14), (1, 27),
    (1, 26), (1, 30), (0, 31), (1, 45), (1, 28), (1, 31), (0, 32), (1, 37), (1, 36), (1, 47),
    (1, 34), (0, 33), (1, 38), (1, 35), (1, 33), (1, 43), (READY, 0), (WORK, 1), (1, 44), (1, 46),
    (WORK, 17), (READY, 1),
)
FIRST, *_, LAST = [k for what, k in ORDER if what == READY]

DIRECT = ()
FAR, NEAR = (4, 5, 6, 7), (3, 2, 1)
FINISH = (4, 5, 6, 7, 0, 3, 2, 1)


class Place:
    def __init__(self):
        o, s = lax.axis_index("opg"), lax.axis_index("sec")
        self.z, self.xl = o // 2, o % 2
        self.xh, self.y, self.c = s // 8, (s // 2) % 4, s % 2
        self.colour = (self.xl + self.xh + self.z) % 2

    def at(self, z=None, xl=None, xh=None, y=None, c=None):
        z = self.z if z is None else z
        xl = self.xl if xl is None else xl
        xh = self.xh if xh is None else xh
        y = self.y if y is None else y
        c = self.c if c is None else c
        return (z * 2 + xl, (xh * 4 + y) * 2 + c)

    def neighbour(self, link):
        if link == YP:
            return self.at(y=(self.y + 1) % 4)
        if link == YM:
            return self.at(y=(self.y + 3) % 4)
        if link == XC:
            return self.at(xl=1 - self.xl, xh=1 - self.xh)
        if link == XP:
            return self.at(xl=1 - self.xl)
        if link == ZP:
            return self.at(z=(self.z + 1) % 8)
        if link == ZM:
            return self.at(z=(self.z + 7) % 8)
        if link == CORE:
            return self.at(c=1 - self.c)
        if link == XPC:
            return self.at(xl=1 - self.xl, c=1 - self.c)
        if link == ZPC:
            return self.at(z=(self.z + 1) % 8, c=1 - self.c)
        assert link == ZMC
        return self.at(z=(self.z + 7) % 8, c=1 - self.c)


def kernel(
    psi, left, right, source_in, coef_index_in, sixj_in, out, gs, source, coef_index, sixj,
    lv, rv, hv, acc, sa, ra, sb, rb, sd, rd, load_sem, send_sem, recv_sem, rs_send, rs_recv,
):
    here = Place()
    group = here.xh * 4 + here.y
    own = group * 4 + here.c * 2
    groups = [x * 4 + (here.y + d) % 4 for x in (here.xh, 1 - here.xh) for d in range(4)]

    loads = [
        pltpu.make_async_copy(
            psi.at[:, :, COLS[k]], gs[k].at[pl.ds(own, 2)], load_sem.at[k]
        )
        for k in range(NCH)
    ]
    tables = [
        pltpu.make_async_copy(source_in, source, load_sem.at[NCH + 2]),
        pltpu.make_async_copy(coef_index_in, coef_index, load_sem.at[NCH + 3]),
        pltpu.make_async_copy(sixj_in, sixj, load_sem.at[NCH + 4]),
    ]
    load_left = pltpu.make_async_copy(left, lv, load_sem.at[NCH])
    load_right = pltpu.make_async_copy(right, rv, load_sem.at[NCH + 1])
    for load in loads:
        load.start()

    barrier = pltpu.get_barrier_semaphore()
    adjacent = [here.neighbour(n) for n in LINKS]
    for device in adjacent:
        pl.semaphore_signal(barrier, inc=1, device_id=device, device_id_type=MESH)
    pl.semaphore_wait(barrier, len(adjacent))

    def message(k, i):
        link, who, lo, hi, sector, _ = MESSAGES[k][i]
        first = groups[who] * 4 + here.c * 2
        if sector == BOTH:
            ref = gs[k].at[pl.ds(first, 2)]
        else:
            sector = first + (here.colour if sector == MINE else 1 - here.colour)
            ref = gs[k].at[sector, pl.ds(lo, hi - lo)]
        return pltpu.make_async_remote_copy(
            src_ref=ref,
            dst_ref=ref,
            send_sem=send_sem.at[k],
            recv_sem=recv_sem.at[k, i],
            device_id=here.neighbour(link),
            device_id_type=MESH,
        )

    arrived = set()

    def arrival(k, i):
        if (k, i) not in arrived:
            arrived.add((k, i))
            message(k, i).wait_recv()

    def first(k, p, s, rows=slice(0, SB)):
        half = jnp.dot(lv[p, s, rows], gs[k][source[s, p]], preferred_element_type=jnp.float32)
        if WIDTHS[k] == 1:
            half = half * sixj[coef_index[s, p]]
        hv[s, p, rows, : 128 * WIDTHS[k]] = half.astype(jnp.bfloat16)

    def times_transposed(a, b):
        return lax.dot_general(a, b, (((1,), (1,)), ((), ())), preferred_element_type=jnp.float32)

    def second(k, s, rows=slice(0, SB), zs=slice(0, 8)):
        halves = [hv[s, p, rows, : 128 * WIDTHS[k]] for p in range(NP)]
        rights = [rv[p, s, :, COLS[k]] for p in range(NP)]
        if WIDTHS[k] == 1:
            part = times_transposed(jnp.concatenate(halves, axis=1), jnp.concatenate(rights, axis=1))
        else:
            part = sum(
                times_transposed(halves[p], rights[p]) * sixj[coef_index[s, p]] for p in range(NP)
            )
        part = part.reshape(-1, 2, ROWS, SB)
        if k == FIRST:
            acc[s, zs] = part
        else:
            acc[s, zs] += part

    mine, theirs = here.xl, 1 - here.xl
    near, low = here.z // 4, here.z % 4
    flips = (low, low + 1 - 2 * (low % 2), (low + 2) % 4, 3 - low)
    places = [4 * near + flips[m] for m in range(4)]
    places += [4 * (1 - near) + flips[m] for m in range(4)]

    def partial_sum(m, whose):
        return jnp.concatenate([acc[s, places[m], whose] for s in range(2)], axis=0)

    def to_partner(m):
        return pltpu.make_async_remote_copy(
            src_ref=sa.at[m],
            dst_ref=ra.at[m],
            send_sem=rs_send.at[0],
            recv_sem=rs_recv.at[m],
            device_id=here.neighbour(XP),
            device_id_type=MESH,
        )

    def along_z(m):
        src, dst = (sd, rd) if m in DIRECT else (sb, rb)
        slot = DIRECT.index(m) if m in DIRECT else m - 1
        return pltpu.make_async_remote_copy(
            src_ref=src.at[slot],
            dst_ref=dst.at[slot],
            send_sem=rs_send.at[2 if m in DIRECT else 1],
            recv_sem=rs_recv.at[8 + m],
            device_id=here.at(z=places[m]),
            device_id_type=MESH,
        )

    def share(m):
        if m in DIRECT:
            both = jnp.concatenate([partial_sum(m, mine), partial_sum(m, theirs)], axis=0)
            sd[DIRECT.index(m)] = both.astype(jnp.bfloat16)
            along_z(m).start()
        else:
            sa[m] = partial_sum(m, theirs).astype(jnp.bfloat16)
            to_partner(m).start()

    def last_tasks(k):
        tasks = []
        for half, ms in ((1 - near, FAR), (near, NEAR)):
            rows = pl.ds(pl.multiple_of(half * (SB // 2), SB // 2), SB // 2)
            zs = pl.ds(half * 4, 4)
            for s in range(2):
                tasks += [functools.partial(first, k, p, s, rows) for p in range(NP)]
                tasks.append(functools.partial(second, k, s, rows, zs))
            tasks += [functools.partial(share, m) for m in ms]
        return tasks

    todo = []
    loaded = set()
    for k, what in ORDER:
        if k == READY:
            if what == FIRST:
                for load in (load_left, load_right, *tables):
                    load.wait()
            for i in range(len(MESSAGES[what])):
                arrival(what, i)
            if what == LAST:
                todo += last_tasks(what)
            else:
                for s in range(2):
                    todo += [functools.partial(first, what, p, s) for p in range(NP)]
                    todo.append(functools.partial(second, what, s))
        elif k == WORK:
            for task in todo[:what]:
                task()
            todo = todo[what:]
        else:
            if k not in loaded:
                loaded.add(k)
                loads[k].wait()
                if len(loaded) == NCH:
                    for load in (load_left, load_right, *tables):
                        load.start()
            for i in MESSAGES[k][what][5]:
                arrival(k, i)
            message(k, what).start()

    for task in todo:
        task()

    total = None
    for m in FINISH:
        if m == 0:
            total = partial_sum(0, mine)
            gift = partial_sum(0, theirs)
            for n in DIRECT:
                along_z(n).wait_recv()
                total = total + rd[DIRECT.index(n), : 2 * ROWS].astype(jnp.float32)
                gift = gift + rd[DIRECT.index(n), 2 * ROWS :].astype(jnp.float32)
            sa[0] = gift.astype(jnp.bfloat16)
            to_partner(0).start()
        else:
            to_partner(m).wait_recv()
            sb[m - 1] = (partial_sum(m, mine) + ra[m].astype(jnp.float32)).astype(jnp.bfloat16)
            along_z(m).start()
    for m in FINISH:
        if m == 0:
            to_partner(0).wait_recv()
            total = total + ra[0].astype(jnp.float32)
        else:
            along_z(m).wait_recv()
            total = total + rb[m - 1].astype(jnp.float32)
    out[...] = total.astype(jnp.bfloat16)

    for k in range(NCH):
        rows = sum((hi - lo) * (2 if sector == BOTH else 1) for _, _, lo, hi, sector, _ in MESSAGES[k])
        assert rows % SB == 0
        ref = gs[k].at[pl.ds(0, rows // SB)]
        pltpu.make_async_copy(ref, ref, send_sem.at[k]).wait()
    sent = [(sa.at[pl.ds(0, 8 - len(DIRECT))], 0), (sb.at[pl.ds(0, 7 - len(DIRECT))], 1)]
    if DIRECT:
        sent.append((sd, 2))
    for ref, i in sent:
        pltpu.make_async_copy(ref, ref, rs_send.at[i]).wait()


def on_device(psi, left_ops, right_ops, source, coef_index, sixj):
    hbm = pl.BlockSpec(memory_space=pltpu.HBM)
    bf16, f32 = jnp.bfloat16, jnp.float32
    mine = pl.pallas_call(
        kernel,
        name="sigma",
        out_shape=jax.ShapeDtypeStruct((2 * ROWS, SB), bf16),
        in_specs=[hbm] * 6,
        out_specs=pl.BlockSpec(memory_space=pltpu.VMEM),
        scratch_shapes=[
            [pltpu.VMEM((32, SB, 128 * w), bf16) for w in WIDTHS],
            pltpu.SMEM((2, NP), jnp.int32),
            pltpu.SMEM((2, NP), jnp.int32),
            pltpu.SMEM((64,), f32),
            pltpu.VMEM((NP, 2, SB, SB), bf16),
            pltpu.VMEM((NP, 2, SB, SB), bf16),
            pltpu.VMEM((2, NP, SB, 128 * max(WIDTHS)), bf16),
            pltpu.VMEM((2, 8, 2, ROWS, SB), f32),
            pltpu.VMEM((8, 2 * ROWS, SB), bf16),
            pltpu.VMEM((8, 2 * ROWS, SB), bf16),
            pltpu.VMEM((7, 2 * ROWS, SB), bf16),
            pltpu.VMEM((7, 2 * ROWS, SB), bf16),
            pltpu.VMEM((max(1, len(DIRECT)), 4 * ROWS, SB), bf16),
            pltpu.VMEM((max(1, len(DIRECT)), 4 * ROWS, SB), bf16),
            pltpu.SemaphoreType.DMA((NCH + 5,)),
            pltpu.SemaphoreType.DMA((NCH,)),
            pltpu.SemaphoreType.DMA((NCH, max(len(table) for table in MESSAGES))),
            pltpu.SemaphoreType.DMA((3,)),
            pltpu.SemaphoreType.DMA((16,)),
        ],
        compiler_params=pltpu.CompilerParams(
            collective_id=0, has_side_effects=True, vmem_limit_bytes=56 * 2**20
        ),
    )(psi, left_ops, right_ops, source.T, coef_index.T, sixj)
    return jnp.transpose(mine.reshape(2, ROWS, SB), (1, 0, 2))


def solution(mesh):
    placed = (
        P("sec", None, None),
        P("opg", "sec", None, None),
        P("opg", "sec", None, None),
        P("opg", "sec"),
        P("opg", "sec"),
        P(),
    )
    return jax.shard_map(
        on_device, mesh=mesh, in_specs=placed, out_specs=P("opg", "sec", None), check_vma=False
    )
```

```python
import functools

import jax
import jax.numpy as jnp
from jax import lax
from jax.experimental import pallas as pl
from jax.experimental.pallas import tpu as pltpu
from jax.sharding import PartitionSpec as P

MESH = pl.DeviceIdType.MESH
SB = 384
WIDTHS = (1, 2)
NCH = len(WIDTHS)
COLS = [slice(128 * sum(WIDTHS[:k]), 128 * sum(WIDTHS[: k + 1])) for k in range(NCH)]
NP = 8
ROWS = 24


YP, YM, XC, XP, ZP, ZM, CORE, XPC, ZPC, ZMC = LINKS = range(10)
OWN, Y1, Y2, Y3, X0, X1, X2, X3 = range(8)
READY, WORK = -1, -2
MINE, OTHER, BOTH = range(3)
MESSAGES = (
    (
        (YM, OWN, 0, 128, MINE, ()),
        (YM, OWN, 128, 384, MINE, ()),
        (YP, OWN, 0, 128, MINE, ()),
        (YP, OWN, 128, 384, MINE, ()),
        (XC, OWN, 0, 384, MINE, ()),
        (YP, Y3, 0, 192, MINE, (2, 3)),
        (YM, Y1, 192, 384, MINE, (1,)),
        (YM, X0, 0, 192, MINE, (4,)),
        (YM, X0, 192, 320, MINE, (4,)),
        (YP, X0, 0, 192, MINE, (4,)),
        (YP, X0, 192, 320, MINE, (4,)),
        (XC, Y1, 320, 384, MINE, (1,)),
        (XC, Y3, 320, 384, MINE, (3,)),
        (XC, Y2, 0, 192, MINE, (5,)),
        (XC, Y2, 192, 384, MINE, (6,)),
        (ZM, Y1, 0, 384, MINE, (0, 1)),
        (ZP, Y3, 0, 384, MINE, (2, 3)),
        (XP, X0, 0, 384, MINE, (4,)),
        (ZP, Y2, 0, 384, MINE, (5, 6)),
        (XP, X1, 0, 384, MINE, (7, 8, 11)),
        (ZM, X3, 0, 192, MINE, (9,)),
        (ZM, X3, 192, 384, MINE, (10, 12)),
        (ZP, X2, 0, 128, MINE, (13,)),
        (XP, X2, 128, 256, MINE, (13, 14)),
        (ZM, X2, 256, 384, MINE, (14,)),
        (CORE, OWN, 0, 384, BOTH, ()),
        (CORE, Y1, 0, 384, BOTH, (0, 1, 15)),
        (CORE, Y3, 0, 384, BOTH, (2, 3, 16)),
        (CORE, X0, 0, 384, BOTH, (4, 17)),
        (CORE, Y2, 0, 384, BOTH, (5, 6, 18)),
        (CORE, X1, 0, 384, BOTH, (7, 8, 11, 19)),
        (CORE, X3, 0, 384, BOTH, (9, 10, 12, 20, 21)),
        (CORE, X2, 0, 384, BOTH, (13, 14, 22, 23, 24)),
    ),
    (
        (YM, OWN, 0, 192, MINE, ()),
        (YM, OWN, 192, 384, MINE, ()),
        (YP, OWN, 0, 192, MINE, ()),
        (YP, OWN, 192, 384, MINE, ()),
        (XC, OWN, 0, 64, MINE, ()),
        (XC, OWN, 64, 384, MINE, ()),
        (YP, Y3, 0, 64, MINE, (2,)),
        (YP, Y3, 64, 192, MINE, (2,)),
        (YM, Y1, 192, 384, MINE, (1,)),
        (YM, X0, 0, 64, MINE, (4,)),
        (YM, X0, 64, 192, MINE, (5,)),
        (YP, X0, 0, 64, MINE, (4,)),
        (YP, X0, 64, 192, MINE, (5,)),
        (XC, Y1, 192, 384, MINE, (1,)),
        (XC, Y3, 192, 384, MINE, (3,)),
        (YM, X1, 0, 64, MINE, (9,)),
        (YM, X1, 64, 128, MINE, (10,)),
        (YP, X3, 256, 384, MINE, (14,)),
        (XC, Y2, 128, 192, MINE, (7,)),
        (XC, Y2, 192, 256, MINE, (8,)),
        (YM, OWN, 0, 192, OTHER, ()),
        (YP, OWN, 0, 192, OTHER, ()),
        (XC, OWN, 0, 64, OTHER, ()),
        (ZP, Y1, 192, 384, MINE, (1,)),
        (ZM, Y3, 192, 384, MINE, (3,)),
        (XP, X0, 64, 384, MINE, (5,)),
        (ZM, Y2, 0, 128, MINE, (6, 7)),
        (XP, Y2, 128, 256, MINE, (7, 8)),
        (ZP, Y2, 256, 384, MINE, (8,)),
        (ZM, X1, 0, 128, MINE, (9, 10)),
        (XP, X1, 128, 256, MINE, (10, 13)),
        (ZP, X1, 256, 384, MINE, (13,)),
        (ZM, X3, 0, 128, MINE, (11, 12)),
        (XP, X3, 128, 256, MINE, (12, 14)),
        (ZP, X3, 256, 384, MINE, (14,)),
        (ZM, X2, 0, 128, MINE, (15, 16)),
        (ZMC, X2, 0, 128, MINE, (15, 16)),
        (XP, X2, 128, 256, MINE, (18, 19)),
        (XPC, X2, 128, 256, MINE, (18, 19)),
        (ZP, X2, 256, 384, MINE, (17,)),
        (ZPC, X2, 256, 384, MINE, (17,)),
        (CORE, OWN, 0, 384, BOTH, ()),
        (CORE, Y1, 0, 384, MINE, (0, 1)),
        (CORE, Y1, 0, 384, OTHER, (20, 23)),
        (CORE, Y3, 0, 384, BOTH, (2, 3, 24, 21)),
        (CORE, X0, 0, 384, BOTH, (4, 5, 25, 22)),
        (CORE, Y2, 0, 384, BOTH, (6, 7, 8, 26, 27, 28)),
        (CORE, X1, 0, 384, MINE, (9, 10, 13)),
        (CORE, X1, 0, 384, OTHER, (29, 30, 31)),
        (CORE, X3, 0, 384, BOTH, (11, 12, 14, 32, 33, 34)),
        (CORE, X2, 0, 384, MINE, (15, 16, 17, 18, 19)),
    ),
)
ORDER = (
    (0, 3), (0, 25), (0, 4), (0, 1), (1, 41), (0, 2), (0, 0), (1, 3), (1, 5), (1, 1), (1, 2),
    (0, 6), (0, 16), (0, 17), (0, 15), (0, 7), (0, 12), (0, 11), (0, 5), (1, 4), (0, 8), (1, 24),
    (1, 23), (1, 14), (1, 8), (0, 9), (1, 25), (0, 10), (0, 27), (0, 28), (1, 12), (0, 14), (1, 10),
    (0, 26), (0, 18), (0, 13), (1, 11), (1, 9), (0, 20), (0, 19), (1, 7), (1, 13), (1, 0), (1, 34),
    (0, 21), (1, 6), (0, 24), (1, 28), (1, 33), (1, 22), (1, 17), (1, 16), (1, 32), (1, 19),
    (0, 29), (1, 15), (0, 22), (0, 23), (1, 21), (1, 29), (1, 20), (1, 18), (1, 27), (0, 31),
    (0, 30), (1, 31), (1, 47), (1, 42), (1, 26), (1, 45), (1, 30), (1, 40), (1, 49), (1, 36),
    (0, 32), (1, 38), (1, 50), (1, 39), (1, 35), (1, 44), (1, 37), (1, 43), (1, 46), (READY, 0),
    (WORK, 2), (1, 48), (WORK, 16), (READY, 1),
)
FIRST, *_, LAST = [k for what, k in ORDER if what == READY]

class Place:
    def __init__(self):
        o, s = lax.axis_index("opg"), lax.axis_index("sec")
        self.z, self.xl = o // 2, o % 2
        self.xh, self.y, self.c = s // 8, (s // 2) % 4, s % 2
        self.colour = (self.xl + self.xh + self.z) % 2

    def at(self, z=None, xl=None, xh=None, y=None, c=None):
        z = self.z if z is None else z
        xl = self.xl if xl is None else xl
        xh = self.xh if xh is None else xh
        y = self.y if y is None else y
        c = self.c if c is None else c
        return (z * 2 + xl, (xh * 4 + y) * 2 + c)

    def neighbour(self, link):
        if link == YP:
            return self.at(y=(self.y + 1) % 4)
        if link == YM:
            return self.at(y=(self.y + 3) % 4)
        if link == XC:
            return self.at(xl=1 - self.xl, xh=1 - self.xh)
        if link == XP:
            return self.at(xl=1 - self.xl)
        if link == ZP:
            return self.at(z=(self.z + 1) % 8)
        if link == ZM:
            return self.at(z=(self.z + 7) % 8)
        if link == CORE:
            return self.at(c=1 - self.c)
        if link == XPC:
            return self.at(xl=1 - self.xl, c=1 - self.c)
        if link == ZPC:
            return self.at(z=(self.z + 1) % 8, c=1 - self.c)
        assert link == ZMC
        return self.at(z=(self.z + 7) % 8, c=1 - self.c)


def kernel(
    psi, left, right, source_in, coef_index_in, sixj_in, out, gs, source, coef_index, sixj,
    lv, rv, hv, acc, sa, ra, sb, load_sem, send_sem, recv_sem, rs_send, rs_recv,
):
    here = Place()
    group = here.xh * 4 + here.y
    own = group * 4 + here.c * 2
    groups = [x * 4 + (here.y + d) % 4 for x in (here.xh, 1 - here.xh) for d in range(4)]

    loads = [
        pltpu.make_async_copy(
            psi.at[:, :, COLS[k]], gs[k].at[pl.ds(own, 2)], load_sem.at[k]
        )
        for k in range(NCH)
    ]
    tables = [
        pltpu.make_async_copy(source_in, source, load_sem.at[NCH + 2]),
        pltpu.make_async_copy(coef_index_in, coef_index, load_sem.at[NCH + 3]),
        pltpu.make_async_copy(sixj_in, sixj, load_sem.at[NCH + 4]),
    ]
    load_left = pltpu.make_async_copy(left, lv, load_sem.at[NCH])
    load_right = pltpu.make_async_copy(right, rv, load_sem.at[NCH + 1])
    for load in loads:
        load.start()

    barrier = pltpu.get_barrier_semaphore()
    adjacent = [here.neighbour(n) for n in LINKS]
    for device in adjacent:
        pl.semaphore_signal(barrier, inc=1, device_id=device, device_id_type=MESH)
    pl.semaphore_wait(barrier, len(adjacent))

    def message(k, i):
        link, who, lo, hi, sector, _ = MESSAGES[k][i]
        first = groups[who] * 4 + here.c * 2
        if sector == BOTH:
            ref = gs[k].at[pl.ds(first, 2)]
        else:
            sector = first + (here.colour if sector == MINE else 1 - here.colour)
            ref = gs[k].at[sector, pl.ds(lo, hi - lo)]
        return pltpu.make_async_remote_copy(
            src_ref=ref,
            dst_ref=ref,
            send_sem=send_sem.at[k],
            recv_sem=recv_sem.at[k, i],
            device_id=here.neighbour(link),
            device_id_type=MESH,
        )

    arrived = set()

    def arrival(k, i):
        if (k, i) not in arrived:
            arrived.add((k, i))
            message(k, i).wait_recv()

    def first(k, p, s, rows=slice(0, SB)):
        half = jnp.dot(lv[p, s, rows], gs[k][source[s, p]], preferred_element_type=jnp.float32)
        if WIDTHS[k] == 1:
            half = half * sixj[coef_index[s, p]]
        hv[s, p, rows, : 128 * WIDTHS[k]] = half.astype(jnp.bfloat16)

    def times_transposed(a, b):
        return lax.dot_general(a, b, (((1,), (1,)), ((), ())), preferred_element_type=jnp.float32)

    def second(k, s, rows=slice(0, SB), zs=slice(0, 8)):
        halves = [hv[s, p, rows, : 128 * WIDTHS[k]] for p in range(NP)]
        rights = [rv[p, s, :, COLS[k]] for p in range(NP)]
        if WIDTHS[k] == 1:
            part = times_transposed(jnp.concatenate(halves, axis=1), jnp.concatenate(rights, axis=1))
        else:
            part = sum(
                times_transposed(halves[p], rights[p]) * sixj[coef_index[s, p]] for p in range(NP)
            )
        part = part.reshape(-1, 2, ROWS, SB)
        if k == FIRST:
            acc[s, zs] = part
        else:
            acc[s, zs] += part

    mine, theirs = here.xl, 1 - here.xl
    near, low = here.z // 4, here.z % 4
    flips = (low, low + 1 - 2 * (low % 2), (low + 2) % 4, 3 - low)
    places = [4 * near + flips[m] for m in range(4)]
    places += [4 * (1 - near) + flips[m] for m in range(4)]

    def partial_sum(m, whose):
        return jnp.concatenate([acc[s, places[m], whose] for s in range(2)], axis=0)

    def to_partner(m):
        return pltpu.make_async_remote_copy(
            src_ref=sa.at[m],
            dst_ref=ra.at[m],
            send_sem=rs_send.at[0],
            recv_sem=rs_recv.at[m],
            device_id=here.neighbour(XP),
            device_id_type=MESH,
        )

    def along_z(m):
        return pltpu.make_async_remote_copy(
            src_ref=sb.at[m],
            dst_ref=out.at[m],
            send_sem=rs_send.at[1],
            recv_sem=rs_recv.at[8 + m],
            device_id=here.at(z=places[m]),
            device_id_type=MESH,
        )

    def share(m):
        sa[m] = partial_sum(m, theirs).astype(jnp.bfloat16)
        to_partner(m).start()

    def last_tasks(k):
        tasks = []
        for z, count, ms in (
            (4 * (1 - near), 4, (4, 5, 6, 7)),
            (4 * near, 4, (3, 2, 1, 0)),
        ):
            n = SB // 8
            rows = pl.ds(pl.multiple_of(z * n, 2 * n), count * n)
            zs = pl.ds(z, count)
            for s in range(2):
                tasks += [functools.partial(first, k, p, s, rows) for p in range(NP)]
                tasks.append(functools.partial(second, k, s, rows, zs))
            tasks += [functools.partial(share, m) for m in ms]
        return tasks

    todo = []
    loaded = set()
    for k, what in ORDER:
        if k == READY:
            if what == FIRST:
                for load in (load_left, load_right, *tables):
                    load.wait()
            for i in range(len(MESSAGES[what])):
                arrival(what, i)
            if what == LAST:
                todo += last_tasks(what)
            else:
                for s in range(2):
                    todo += [functools.partial(first, what, p, s) for p in range(NP)]
                    todo.append(functools.partial(second, what, s))
        elif k == WORK:
            for task in todo[:what]:
                task()
            todo = todo[what:]
        else:
            if k not in loaded:
                loaded.add(k)
                loads[k].wait()
                if len(loaded) == NCH:
                    for load in (load_left, load_right, *tables):
                        load.start()
            for i in MESSAGES[k][what][5]:
                arrival(k, i)
            message(k, what).start()

    for task in todo:
        task()

    for m in (4, 5, 6, 7, 3, 2, 1):
        to_partner(m).wait_recv()
        sb[m] = (partial_sum(m, mine) + ra[m].astype(jnp.float32)).astype(jnp.bfloat16)
        along_z(m).start()
    to_partner(0).wait_recv()
    sb[0] = (partial_sum(0, mine) + ra[0].astype(jnp.float32)).astype(jnp.bfloat16)
    keep = pltpu.make_async_copy(sb.at[0], out.at[0], rs_recv.at[8])
    keep.start()
    for m in (4, 5, 6, 7, 3, 2, 1):
        along_z(m).wait_recv()
    keep.wait()

    rb = sb.at[pl.ds(0, 7)]
    for k in range(NCH):
        rows = sum((hi - lo) * (2 if sector == BOTH else 1) for _, _, lo, hi, sector, _ in MESSAGES[k])
        assert rows % SB == 0
        ref = gs[k].at[pl.ds(0, rows // SB)]
        pltpu.make_async_copy(ref, ref, send_sem.at[k]).wait()
    pltpu.make_async_copy(sa, sa, rs_send.at[0]).wait()
    pltpu.make_async_copy(rb, rb, rs_send.at[1]).wait()


def on_device(psi, left_ops, right_ops, source, coef_index, sixj):
    hbm = pl.BlockSpec(memory_space=pltpu.HBM)
    bf16, f32 = jnp.bfloat16, jnp.float32
    parts = pl.pallas_call(
        kernel,
        name="sigma",
        out_shape=jax.ShapeDtypeStruct((8, 2 * ROWS, SB), bf16),
        in_specs=[hbm] * 6,
        out_specs=pl.BlockSpec(memory_space=pl.ANY),
        scratch_shapes=[
            [pltpu.VMEM((32, SB, 128 * w), bf16) for w in WIDTHS],
            pltpu.SMEM((2, NP), jnp.int32),
            pltpu.SMEM((2, NP), jnp.int32),
            pltpu.SMEM((64,), f32),
            pltpu.VMEM((NP, 2, SB, SB), bf16),
            pltpu.VMEM((NP, 2, SB, SB), bf16),
            pltpu.VMEM((2, NP, SB, 128 * max(WIDTHS)), bf16),
            pltpu.VMEM((2, 8, 2, ROWS, SB), f32),
            pltpu.VMEM((8, 2 * ROWS, SB), bf16),
            pltpu.VMEM((8, 2 * ROWS, SB), bf16),
            pltpu.VMEM((8, 2 * ROWS, SB), bf16),
            pltpu.SemaphoreType.DMA((NCH + 5,)),
            pltpu.SemaphoreType.DMA((NCH,)),
            pltpu.SemaphoreType.DMA((NCH, max(len(table) for table in MESSAGES))),
            pltpu.SemaphoreType.DMA((2,)),
            pltpu.SemaphoreType.DMA((16,)),
        ],
        compiler_params=pltpu.CompilerParams(
            collective_id=0, has_side_effects=True, vmem_limit_bytes=56 * 2**20
        ),
    )(psi, left_ops, right_ops, source.T, coef_index.T, sixj)
    mine = jnp.sum(parts.astype(f32), axis=0).astype(bf16)
    return jnp.transpose(mine.reshape(2, ROWS, SB), (1, 0, 2))


def solution(mesh):
    placed = (
        P("sec", None, None),
        P("opg", "sec", None, None),
        P("opg", "sec", None, None),
        P("opg", "sec"),
        P("opg", "sec"),
        P(),
    )
    return jax.shard_map(
        on_device, mesh=mesh, in_specs=placed, out_specs=P("opg", "sec", None), check_vma=False
    )
```

```python
import functools

import jax
import jax.numpy as jnp
from jax import lax
from jax.experimental import pallas as pl
from jax.experimental.pallas import tpu as pltpu
from jax.sharding import PartitionSpec as P

MESH = pl.DeviceIdType.MESH
SB = 384
WIDTHS = (2, 1)
NCH = len(WIDTHS)
COLS = [slice(128 * sum(WIDTHS[:k]), 128 * sum(WIDTHS[: k + 1])) for k in range(NCH)]
NP = 8
ROWS = 24


YP, YM, XC, XP, ZP, ZM, CORE, XPC, ZPC, ZMC = LINKS = range(10)
OWN, Y1, Y2, Y3, X0, X1, X2, X3 = range(8)
READY, WORK = -1, -2
MINE, OTHER, BOTH = range(3)
MESSAGES = (
    (
        (YM, OWN, 0, 192, MINE, ()),
        (YM, OWN, 192, 384, MINE, ()),
        (YP, OWN, 0, 192, MINE, ()),
        (YP, OWN, 192, 384, MINE, ()),
        (XC, OWN, 0, 256, MINE, ()),
        (XC, OWN, 256, 384, MINE, ()),
        (YP, Y3, 0, 128, MINE, (2,)),
        (YP, Y3, 128, 192, MINE, (2,)),
        (YM, Y1, 192, 256, MINE, (1,)),
        (YM, Y1, 256, 384, MINE, (1,)),
        (YM, X0, 0, 192, MINE, (4,)),
        (YP, X0, 0, 192, MINE, (4,)),
        (XC, Y1, 192, 384, MINE, (1,)),
        (XC, Y3, 192, 384, MINE, (3,)),
        (YM, X1, 0, 128, MINE, (10,)),
        (YP, X3, 256, 384, MINE, (13,)),
        (XC, Y2, 128, 192, MINE, (7,)),
        (XC, Y2, 192, 256, MINE, (8,)),
        (YM, OWN, 0, 192, OTHER, ()),
        (YP, OWN, 0, 192, OTHER, ()),
        (XP, Y1, 192, 384, MINE, (1,)),
        (ZP, Y3, 192, 384, MINE, (3,)),
        (ZM, X0, 0, 128, MINE, (4,)),
        (XP, X0, 128, 256, MINE, (4,)),
        (ZP, X0, 256, 384, MINE, (5,)),
        (ZM, Y2, 0, 128, MINE, (6,)),
        (XP, Y2, 128, 256, MINE, (7, 8)),
        (ZP, Y2, 256, 384, MINE, (9,)),
        (ZM, X1, 0, 128, MINE, (10,)),
        (XP, X1, 128, 256, MINE, (10, 12)),
        (ZP, X1, 256, 384, MINE, (12,)),
        (ZM, X3, 0, 256, MINE, (11, 13)),
        (ZM, X3, 256, 384, MINE, (13,)),
        (ZM, X2, 0, 128, MINE, (14,)),
        (ZMC, X2, 0, 128, MINE, (14,)),
        (XP, X2, 128, 256, MINE, (16, 17)),
        (XPC, X2, 128, 256, MINE, (16, 17)),
        (ZP, X2, 256, 384, MINE, (15,)),
        (ZPC, X2, 256, 384, MINE, (15,)),
        (CORE, OWN, 0, 384, BOTH, ()),
        (CORE, Y1, 0, 384, MINE, (0, 1)),
        (CORE, Y1, 0, 384, OTHER, (18, 20)),
        (CORE, Y3, 0, 384, MINE, (2, 3)),
        (CORE, Y3, 0, 384, OTHER, (19, 21)),
        (CORE, X0, 0, 384, BOTH, (4, 5, 22, 23, 24)),
        (CORE, Y2, 0, 384, MINE, (6, 7, 8, 9)),
        (CORE, Y2, 0, 384, OTHER, (25, 26, 27)),
        (CORE, X1, 0, 384, MINE, (10, 12)),
        (CORE, X1, 0, 384, OTHER, (28, 29, 30)),
        (CORE, X3, 0, 384, BOTH, (11, 13, 31, 32)),
        (CORE, X2, 0, 384, MINE, (14, 15, 16, 17)),
    ),
    (
        (YM, OWN, 0, 192, MINE, ()),
        (YM, OWN, 192, 384, MINE, ()),
        (YP, OWN, 0, 192, MINE, ()),
        (YP, OWN, 192, 384, MINE, ()),
        (XC, OWN, 0, 320, MINE, ()),
        (XC, OWN, 320, 384, MINE, ()),
        (YP, Y3, 0, 192, MINE, (2,)),
        (YM, Y1, 192, 384, MINE, (1,)),
        (YM, X0, 0, 320, MINE, (4,)),
        (YP, X0, 0, 320, MINE, (4,)),
        (XC, Y1, 320, 384, MINE, (1,)),
        (XC, Y3, 320, 384, MINE, (3,)),
        (XC, Y2, 0, 64, MINE, (6,)),
        (XC, Y2, 64, 192, MINE, (6,)),
        (XC, Y2, 192, 384, MINE, (7,)),
        (YM, OWN, 0, 64, OTHER, ()),
        (YP, OWN, 0, 64, OTHER, ()),
        (ZM, Y1, 64, 384, MINE, (0, 1)),
        (ZP, Y3, 64, 384, MINE, (2, 3)),
        (ZM, X0, 0, 320, MINE, (4,)),
        (ZM, X0, 320, 384, MINE, (5,)),
        (XP, Y2, 0, 384, MINE, (6, 7)),
        (ZP, X1, 0, 384, MINE, (8, 10)),
        (XP, X3, 0, 384, MINE, (9, 11)),
        (XP, X2, 0, 128, MINE, (12, 13)),
        (ZP, X2, 128, 256, MINE, (13, 14)),
        (ZM, X2, 256, 384, MINE, (14,)),
        (CORE, OWN, 0, 384, BOTH, ()),
        (CORE, Y1, 0, 384, BOTH, (0, 1, 17, 15)),
        (CORE, Y3, 0, 384, BOTH, (2, 3, 18, 16)),
        (CORE, X0, 0, 384, BOTH, (4, 5, 19, 20)),
        (CORE, Y2, 0, 384, BOTH, (6, 7, 21)),
        (CORE, X1, 0, 384, BOTH, (8, 10, 22)),
        (CORE, X3, 0, 384, BOTH, (9, 11, 23)),
        (CORE, X2, 0, 384, BOTH, (12, 13, 14, 24, 25, 26)),
    ),
)
ORDER = (
    (0, 4), (1, 1), (1, 2), (1, 27), (0, 39), (1, 0), (1, 3), (1, 15), (0, 3), (0, 1), (1, 4),
    (1, 6), (0, 5), (1, 7), (1, 17), (1, 18), (0, 2), (0, 23), (0, 10), (1, 5), (0, 22), (1, 11),
    (1, 10), (0, 13), (0, 21), (1, 9), (1, 19), (0, 20), (1, 8), (0, 24), (1, 21), (1, 14), (0, 11),
    (1, 28), (1, 20), (0, 8), (1, 13), (0, 9), (0, 42), (0, 28), (1, 12), (0, 7), (0, 12), (0, 0),
    (0, 6), (0, 32), (1, 23), (1, 22), (1, 30), (0, 44), (1, 26), (1, 16), (0, 17), (0, 14),
    (0, 15), (1, 25), (1, 31), (0, 31), (1, 24), (0, 27), (0, 26), (0, 16), (0, 18), (0, 19),
    (0, 45), (0, 25), (0, 29), (0, 30), (1, 33), (0, 47), (1, 29), (0, 40), (1, 32), (1, 34),
    (0, 35), (0, 33), (0, 37), (0, 50), (0, 36), (0, 38), (0, 34), (0, 49), (0, 41), (0, 43),
    (0, 48), (READY, 1), (WORK, 1), (0, 46), (WORK, 17), (READY, 0),
)
FIRST, *_, LAST = [k for what, k in ORDER if what == READY]

class Place:
    def __init__(self):
        o, s = lax.axis_index("opg"), lax.axis_index("sec")
        self.z, self.xl = o // 2, o % 2
        self.xh, self.y, self.c = s // 8, (s // 2) % 4, s % 2
        self.colour = (self.xl + self.xh + self.z) % 2

    def at(self, z=None, xl=None, xh=None, y=None, c=None):
        z = self.z if z is None else z
        xl = self.xl if xl is None else xl
        xh = self.xh if xh is None else xh
        y = self.y if y is None else y
        c = self.c if c is None else c
        return (z * 2 + xl, (xh * 4 + y) * 2 + c)

    def neighbour(self, link):
        if link == YP:
            return self.at(y=(self.y + 1) % 4)
        if link == YM:
            return self.at(y=(self.y + 3) % 4)
        if link == XC:
            return self.at(xl=1 - self.xl, xh=1 - self.xh)
        if link == XP:
            return self.at(xl=1 - self.xl)
        if link == ZP:
            return self.at(z=(self.z + 1) % 8)
        if link == ZM:
            return self.at(z=(self.z + 7) % 8)
        if link == CORE:
            return self.at(c=1 - self.c)
        if link == XPC:
            return self.at(xl=1 - self.xl, c=1 - self.c)
        if link == ZPC:
            return self.at(z=(self.z + 1) % 8, c=1 - self.c)
        assert link == ZMC
        return self.at(z=(self.z + 7) % 8, c=1 - self.c)


def kernel(
    psi, left, right, source_in, coef_index_in, sixj_in, out, gs, source, coef_index, sixj,
    lv, rv, hv, acc, sa, ra, sb, load_sem, send_sem, recv_sem, rs_send, rs_recv,
):
    here = Place()
    group = here.xh * 4 + here.y
    own = group * 4 + here.c * 2
    groups = [x * 4 + (here.y + d) % 4 for x in (here.xh, 1 - here.xh) for d in range(4)]

    loads = [
        pltpu.make_async_copy(
            psi.at[:, :, COLS[k]], gs[k].at[pl.ds(own, 2)], load_sem.at[k]
        )
        for k in range(NCH)
    ]
    tables = [
        pltpu.make_async_copy(source_in, source, load_sem.at[NCH + 2]),
        pltpu.make_async_copy(coef_index_in, coef_index, load_sem.at[NCH + 3]),
        pltpu.make_async_copy(sixj_in, sixj, load_sem.at[NCH + 4]),
    ]
    load_left = pltpu.make_async_copy(left, lv, load_sem.at[NCH])
    load_right = pltpu.make_async_copy(right, rv, load_sem.at[NCH + 1])

    barrier = pltpu.get_barrier_semaphore()
    adjacent = [here.neighbour(n) for n in LINKS]
    for device in adjacent:
        pl.semaphore_signal(barrier, inc=1, device_id=device, device_id_type=MESH)
    for load in loads:
        load.start()
    pl.semaphore_wait(barrier, len(adjacent))

    def message(k, i):
        link, who, lo, hi, sector, _ = MESSAGES[k][i]
        first = groups[who] * 4 + here.c * 2
        if sector == BOTH:
            ref = gs[k].at[pl.ds(first, 2)]
        else:
            sector = first + (here.colour if sector == MINE else 1 - here.colour)
            ref = gs[k].at[sector, pl.ds(lo, hi - lo)]
        return pltpu.make_async_remote_copy(
            src_ref=ref,
            dst_ref=ref,
            send_sem=send_sem.at[k],
            recv_sem=recv_sem.at[k, i],
            device_id=here.neighbour(link),
            device_id_type=MESH,
        )

    arrived = set()

    def arrival(k, i):
        if (k, i) not in arrived:
            arrived.add((k, i))
            message(k, i).wait_recv()

    def first(k, p, s, rows=slice(0, SB)):
        half = jnp.dot(lv[p, s, rows], gs[k][source[s, p]], preferred_element_type=jnp.float32)
        if WIDTHS[k] == 1:
            half = half * sixj[coef_index[s, p]]
        hv[s, p, rows, : 128 * WIDTHS[k]] = half.astype(jnp.bfloat16)

    def times_transposed(a, b):
        return lax.dot_general(a, b, (((1,), (1,)), ((), ())), preferred_element_type=jnp.float32)

    def second(k, s, rows=slice(0, SB), zs=slice(0, 8)):
        halves = [hv[s, p, rows, : 128 * WIDTHS[k]] for p in range(NP)]
        rights = [rv[p, s, :, COLS[k]] for p in range(NP)]
        if WIDTHS[k] == 1:
            part = times_transposed(jnp.concatenate(halves, axis=1), jnp.concatenate(rights, axis=1))
        else:
            part = sum(
                times_transposed(halves[p], rights[p]) * sixj[coef_index[s, p]] for p in range(NP)
            )
        part = part.reshape(-1, 2, ROWS, SB)
        if k == FIRST:
            acc[s, zs] = part
        else:
            acc[s, zs] += part

    mine, theirs = here.xl, 1 - here.xl
    near, low = here.z // 4, here.z % 4
    flips = (low, low + 1 - 2 * (low % 2), (low + 2) % 4, 3 - low)
    places = [4 * near + flips[m] for m in range(4)]
    places += [4 * (1 - near) + flips[m] for m in range(4)]

    def partial_sum(m, whose):
        return jnp.concatenate([acc[s, places[m], whose] for s in range(2)], axis=0)

    def to_partner(m):
        return pltpu.make_async_remote_copy(
            src_ref=sa.at[m],
            dst_ref=ra.at[m],
            send_sem=rs_send.at[0],
            recv_sem=rs_recv.at[m],
            device_id=here.neighbour(XP),
            device_id_type=MESH,
        )

    def along_z(m):
        return pltpu.make_async_remote_copy(
            src_ref=sb.at[m],
            dst_ref=out.at[m],
            send_sem=rs_send.at[1],
            recv_sem=rs_recv.at[8 + m],
            device_id=here.at(z=places[m]),
            device_id_type=MESH,
        )

    def share(m):
        sa[m] = partial_sum(m, theirs).astype(jnp.bfloat16)
        to_partner(m).start()

    def last_tasks(k):
        tasks = []
        for z, count, ms in (
            (4 * (1 - near), 4, (4, 5, 6, 7)),
            (4 * near, 4, (3, 2, 1, 0)),
        ):
            n = SB // 8
            rows = pl.ds(pl.multiple_of(z * n, 2 * n), count * n)
            zs = pl.ds(z, count)
            for s in range(2):
                tasks += [functools.partial(first, k, p, s, rows) for p in range(NP)]
                tasks.append(functools.partial(second, k, s, rows, zs))
            tasks += [functools.partial(share, m) for m in ms]
        return tasks

    todo = []
    loaded = set()
    for k, what in ORDER:
        if k == READY:
            if what == FIRST:
                for load in (load_left, load_right, *tables):
                    load.wait()
            for i in range(len(MESSAGES[what])):
                arrival(what, i)
            if what == LAST:
                todo += last_tasks(what)
            else:
                for s in range(2):
                    todo += [functools.partial(first, what, p, s) for p in range(NP)]
                    todo.append(functools.partial(second, what, s))
        elif k == WORK:
            for task in todo[:what]:
                task()
            todo = todo[what:]
        else:
            if k not in loaded:
                loaded.add(k)
                loads[k].wait()
                if len(loaded) == NCH:
                    for load in (load_left, load_right, *tables):
                        load.start()
            for i in MESSAGES[k][what][5]:
                arrival(k, i)
            message(k, what).start()

    for task in todo:
        task()

    for m in (4, 5, 6, 7, 3, 2, 1):
        to_partner(m).wait_recv()
        sb[m] = (partial_sum(m, mine) + ra[m].astype(jnp.float32)).astype(jnp.bfloat16)
        along_z(m).start()
    to_partner(0).wait_recv()
    sb[0] = (partial_sum(0, mine) + ra[0].astype(jnp.float32)).astype(jnp.bfloat16)
    keep = pltpu.make_async_copy(sb.at[0], out.at[0], rs_recv.at[8])
    keep.start()
    for m in (4, 5, 6, 7, 3, 2, 1):
        along_z(m).wait_recv()
    keep.wait()

    rb = sb.at[pl.ds(0, 7)]
    for k in range(NCH):
        rows = sum((hi - lo) * (2 if sector == BOTH else 1) for _, _, lo, hi, sector, _ in MESSAGES[k])
        assert rows % SB == 0
        ref = gs[k].at[pl.ds(0, rows // SB)]
        pltpu.make_async_copy(ref, ref, send_sem.at[k]).wait()
    pltpu.make_async_copy(sa, sa, rs_send.at[0]).wait()
    pltpu.make_async_copy(rb, rb, rs_send.at[1]).wait()


def on_device(psi, left_ops, right_ops, source, coef_index, sixj):
    hbm = pl.BlockSpec(memory_space=pltpu.HBM)
    bf16, f32 = jnp.bfloat16, jnp.float32
    parts = pl.pallas_call(
        kernel,
        name="sigma",
        out_shape=jax.ShapeDtypeStruct((8, 2 * ROWS, SB), bf16),
        in_specs=[hbm] * 6,
        out_specs=pl.BlockSpec(memory_space=pl.ANY),
        scratch_shapes=[
            [pltpu.VMEM((32, SB, 128 * w), bf16) for w in WIDTHS],
            pltpu.SMEM((2, NP), jnp.int32),
            pltpu.SMEM((2, NP), jnp.int32),
            pltpu.SMEM((64,), f32),
            pltpu.VMEM((NP, 2, SB, SB), bf16),
            pltpu.VMEM((NP, 2, SB, SB), bf16),
            pltpu.VMEM((2, NP, SB, 128 * max(WIDTHS)), bf16),
            pltpu.VMEM((2, 8, 2, ROWS, SB), f32),
            pltpu.VMEM((8, 2 * ROWS, SB), bf16),
            pltpu.VMEM((8, 2 * ROWS, SB), bf16),
            pltpu.VMEM((8, 2 * ROWS, SB), bf16),
            pltpu.SemaphoreType.DMA((NCH + 5,)),
            pltpu.SemaphoreType.DMA((NCH,)),
            pltpu.SemaphoreType.DMA((NCH, max(len(table) for table in MESSAGES))),
            pltpu.SemaphoreType.DMA((2,)),
            pltpu.SemaphoreType.DMA((16,)),
        ],
        compiler_params=pltpu.CompilerParams(
            collective_id=0, has_side_effects=True, vmem_limit_bytes=56 * 2**20
        ),
    )(psi, left_ops, right_ops, source.T, coef_index.T, sixj)
    mine = jnp.sum(parts.astype(f32), axis=0).astype(bf16)
    return jnp.transpose(mine.reshape(2, ROWS, SB), (1, 0, 2))


def solution(mesh):
    placed = (
        P("sec", None, None),
        P("opg", "sec", None, None),
        P("opg", "sec", None, None),
        P("opg", "sec"),
        P("opg", "sec"),
        P(),
    )
    return jax.shard_map(
        on_device, mesh=mesh, in_specs=placed, out_specs=P("opg", "sec", None), check_vma=False
    )
```

```python
import functools

import jax
import jax.numpy as jnp
from jax import lax
from jax.experimental import pallas as pl
from jax.experimental.pallas import tpu as pltpu
from jax.sharding import PartitionSpec as P

MESH = pl.DeviceIdType.MESH
SB = 384
WIDTHS = (2, 1)
NCH = len(WIDTHS)
COLS = [slice(128 * sum(WIDTHS[:k]), 128 * sum(WIDTHS[: k + 1])) for k in range(NCH)]
NP = 8
ROWS = 24


YP, YM, XC, XP, ZP, ZM, CORE, XPC, ZPC, ZMC = LINKS = range(10)
OWN, Y1, Y2, Y3, X0, X1, X2, X3 = range(8)
READY, WORK = -1, -2
MINE, OTHER, BOTH = range(3)
MESSAGES = (
    (
        (YM, OWN, 0, 192, MINE, ()),
        (YM, OWN, 192, 384, MINE, ()),
        (YP, OWN, 0, 192, MINE, ()),
        (YP, OWN, 192, 384, MINE, ()),
        (XC, OWN, 0, 256, MINE, ()),
        (XC, OWN, 256, 384, MINE, ()),
        (YP, Y3, 0, 128, MINE, (2,)),
        (YP, Y3, 128, 192, MINE, (2,)),
        (YM, Y1, 192, 256, MINE, (1,)),
        (YM, Y1, 256, 384, MINE, (1,)),
        (YM, X0, 0, 192, MINE, (4,)),
        (YP, X0, 0, 192, MINE, (4,)),
        (XC, Y1, 192, 384, MINE, (1,)),
        (XC, Y3, 192, 384, MINE, (3,)),
        (YM, X1, 0, 128, MINE, (10,)),
        (YP, X3, 256, 384, MINE, (13,)),
        (XC, Y2, 128, 192, MINE, (7,)),
        (XC, Y2, 192, 256, MINE, (8,)),
        (YM, OWN, 0, 192, OTHER, ()),
        (YP, OWN, 0, 192, OTHER, ()),
        (XP, Y1, 192, 384, MINE, (1,)),
        (ZP, Y3, 192, 384, MINE, (3,)),
        (ZM, X0, 0, 128, MINE, (4,)),
        (XP, X0, 128, 256, MINE, (4,)),
        (ZP, X0, 256, 384, MINE, (5,)),
        (ZM, Y2, 0, 128, MINE, (6,)),
        (XP, Y2, 128, 256, MINE, (7, 8)),
        (ZP, Y2, 256, 384, MINE, (9,)),
        (ZM, X1, 0, 128, MINE, (10,)),
        (XP, X1, 128, 256, MINE, (10, 12)),
        (ZP, X1, 256, 384, MINE, (12,)),
        (ZM, X3, 0, 256, MINE, (11, 13)),
        (ZM, X3, 256, 384, MINE, (13,)),
        (ZM, X2, 0, 128, MINE, (14,)),
        (ZMC, X2, 0, 128, MINE, (14,)),
        (XP, X2, 128, 256, MINE, (16, 17)),
        (XPC, X2, 128, 256, MINE, (16, 17)),
        (ZP, X2, 256, 384, MINE, (15,)),
        (ZPC, X2, 256, 384, MINE, (15,)),
        (CORE, OWN, 0, 384, BOTH, ()),
        (CORE, Y1, 0, 384, MINE, (0, 1)),
        (CORE, Y1, 0, 384, OTHER, (18, 20)),
        (CORE, Y3, 0, 384, MINE, (2, 3)),
        (CORE, Y3, 0, 384, OTHER, (19, 21)),
        (CORE, X0, 0, 384, BOTH, (4, 5, 22, 23, 24)),
        (CORE, Y2, 0, 384, MINE, (6, 7, 8, 9)),
        (CORE, Y2, 0, 384, OTHER, (25, 26, 27)),
        (CORE, X1, 0, 384, MINE, (10, 12)),
        (CORE, X1, 0, 384, OTHER, (28, 29, 30)),
        (CORE, X3, 0, 384, BOTH, (11, 13, 31, 32)),
        (CORE, X2, 0, 384, MINE, (14, 15, 16, 17)),
    ),
    (
        (YM, OWN, 0, 192, MINE, ()),
        (YM, OWN, 192, 384, MINE, ()),
        (YP, OWN, 0, 192, MINE, ()),
        (YP, OWN, 192, 384, MINE, ()),
        (XC, OWN, 0, 320, MINE, ()),
        (XC, OWN, 320, 384, MINE, ()),
        (YP, Y3, 0, 192, MINE, (2,)),
        (YM, Y1, 192, 384, MINE, (1,)),
        (YM, X0, 0, 320, MINE, (4,)),
        (YP, X0, 0, 320, MINE, (4,)),
        (XC, Y1, 320, 384, MINE, (1,)),
        (XC, Y3, 320, 384, MINE, (3,)),
        (XC, Y2, 0, 64, MINE, (6,)),
        (XC, Y2, 64, 192, MINE, (6,)),
        (XC, Y2, 192, 384, MINE, (7,)),
        (YM, OWN, 0, 64, OTHER, ()),
        (YP, OWN, 0, 64, OTHER, ()),
        (ZM, Y1, 64, 384, MINE, (0, 1)),
        (ZP, Y3, 64, 384, MINE, (2, 3)),
        (ZM, X0, 0, 320, MINE, (4,)),
        (ZM, X0, 320, 384, MINE, (5,)),
        (XP, Y2, 0, 384, MINE, (6, 7)),
        (ZP, X1, 0, 384, MINE, (8, 10)),
        (XP, X3, 0, 384, MINE, (9, 11)),
        (XP, X2, 0, 128, MINE, (12, 13)),
        (ZP, X2, 128, 256, MINE, (13, 14)),
        (ZM, X2, 256, 384, MINE, (14,)),
        (CORE, OWN, 0, 384, BOTH, ()),
        (CORE, Y1, 0, 384, BOTH, (0, 1, 17, 15)),
        (CORE, Y3, 0, 384, BOTH, (2, 3, 18, 16)),
        (CORE, X0, 0, 384, BOTH, (4, 5, 19, 20)),
        (CORE, Y2, 0, 384, BOTH, (6, 7, 21)),
        (CORE, X1, 0, 384, BOTH, (8, 10, 22)),
        (CORE, X3, 0, 384, BOTH, (9, 11, 23)),
        (CORE, X2, 0, 384, BOTH, (12, 13, 14, 24, 25, 26)),
    ),
)
ORDER = (
    (1, 1), (1, 2), (0, 4), (1, 27), (0, 39), (1, 0), (1, 3), (1, 15), (0, 3), (0, 1), (1, 4),
    (1, 6), (0, 5), (1, 7), (1, 17), (1, 18), (0, 2), (0, 23), (0, 10), (1, 5), (0, 22), (1, 11),
    (1, 10), (0, 13), (0, 21), (1, 9), (1, 19), (0, 20), (1, 8), (0, 24), (1, 21), (1, 14), (0, 11),
    (1, 28), (1, 20), (0, 8), (1, 13), (0, 9), (0, 42), (0, 28), (1, 12), (0, 7), (0, 12), (0, 0),
    (0, 6), (0, 32), (1, 23), (1, 22), (1, 30), (0, 44), (1, 26), (1, 16), (0, 17), (0, 14),
    (0, 15), (1, 25), (1, 31), (0, 31), (1, 24), (0, 27), (0, 26), (0, 16), (0, 18), (0, 19),
    (0, 45), (0, 25), (0, 29), (0, 30), (1, 33), (0, 47), (1, 29), (0, 40), (1, 32), (1, 34),
    (0, 35), (0, 33), (0, 37), (0, 50), (0, 36), (0, 38), (0, 34), (0, 49), (0, 41), (0, 43),
    (0, 48), (READY, 1), (WORK, 1), (0, 46), (WORK, 17), (READY, 0),
)
FIRST, *_, LAST = [k for what, k in ORDER if what == READY]

class Place:
    def __init__(self):
        o, s = lax.axis_index("opg"), lax.axis_index("sec")
        self.z, self.xl = o // 2, o % 2
        self.xh, self.y, self.c = s // 8, (s // 2) % 4, s % 2
        self.colour = (self.xl + self.xh + self.z) % 2

    def at(self, z=None, xl=None, xh=None, y=None, c=None):
        z = self.z if z is None else z
        xl = self.xl if xl is None else xl
        xh = self.xh if xh is None else xh
        y = self.y if y is None else y
        c = self.c if c is None else c
        return (z * 2 + xl, (xh * 4 + y) * 2 + c)

    def neighbour(self, link):
        if link == YP:
            return self.at(y=(self.y + 1) % 4)
        if link == YM:
            return self.at(y=(self.y + 3) % 4)
        if link == XC:
            return self.at(xl=1 - self.xl, xh=1 - self.xh)
        if link == XP:
            return self.at(xl=1 - self.xl)
        if link == ZP:
            return self.at(z=(self.z + 1) % 8)
        if link == ZM:
            return self.at(z=(self.z + 7) % 8)
        if link == CORE:
            return self.at(c=1 - self.c)
        if link == XPC:
            return self.at(xl=1 - self.xl, c=1 - self.c)
        if link == ZPC:
            return self.at(z=(self.z + 1) % 8, c=1 - self.c)
        assert link == ZMC
        return self.at(z=(self.z + 7) % 8, c=1 - self.c)


def kernel(
    psi, left, right, source_in, coef_index_in, sixj_in, out, gs, source, coef_index, sixj,
    lv, rv, hv, acc, sa, ra, sb, load_sem, send_sem, recv_sem, rs_send, rs_recv,
):
    here = Place()
    group = here.xh * 4 + here.y
    own = group * 4 + here.c * 2
    groups = [x * 4 + (here.y + d) % 4 for x in (here.xh, 1 - here.xh) for d in range(4)]

    loads = [
        pltpu.make_async_copy(
            psi.at[:, :, COLS[k]], gs[k].at[pl.ds(own, 2)], load_sem.at[k]
        )
        for k in range(NCH)
    ]
    tables = [
        pltpu.make_async_copy(source_in, source, load_sem.at[NCH + 2]),
        pltpu.make_async_copy(coef_index_in, coef_index, load_sem.at[NCH + 3]),
        pltpu.make_async_copy(sixj_in, sixj, load_sem.at[NCH + 4]),
    ]
    load_left = pltpu.make_async_copy(left, lv, load_sem.at[NCH])
    load_right = pltpu.make_async_copy(right, rv, load_sem.at[NCH + 1])

    barrier = pltpu.get_barrier_semaphore()
    adjacent = [here.neighbour(n) for n in LINKS]
    for device in adjacent:
        pl.semaphore_signal(barrier, inc=1, device_id=device, device_id_type=MESH)
    for k in dict.fromkeys(k for k, _ in ORDER if k >= 0):
        loads[k].start()
    pl.semaphore_wait(barrier, len(adjacent))

    def message(k, i):
        link, who, lo, hi, sector, _ = MESSAGES[k][i]
        first = groups[who] * 4 + here.c * 2
        if sector == BOTH:
            ref = gs[k].at[pl.ds(first, 2)]
        else:
            sector = first + (here.colour if sector == MINE else 1 - here.colour)
            ref = gs[k].at[sector, pl.ds(lo, hi - lo)]
        return pltpu.make_async_remote_copy(
            src_ref=ref,
            dst_ref=ref,
            send_sem=send_sem.at[k],
            recv_sem=recv_sem.at[k, i],
            device_id=here.neighbour(link),
            device_id_type=MESH,
        )

    arrived = set()

    def arrival(k, i):
        if (k, i) not in arrived:
            arrived.add((k, i))
            message(k, i).wait_recv()

    def first(k, p, s, rows=slice(0, SB)):
        half = jnp.dot(lv[p, s, rows], gs[k][source[s, p]], preferred_element_type=jnp.float32)
        if WIDTHS[k] == 1:
            half = half * sixj[coef_index[s, p]]
        hv[s, p, rows, : 128 * WIDTHS[k]] = half.astype(jnp.bfloat16)

    def times_transposed(a, b):
        return lax.dot_general(a, b, (((1,), (1,)), ((), ())), preferred_element_type=jnp.float32)

    def second(k, s, rows=slice(0, SB), zs=slice(0, 8)):
        halves = [hv[s, p, rows, : 128 * WIDTHS[k]] for p in range(NP)]
        rights = [rv[p, s, :, COLS[k]] for p in range(NP)]
        if WIDTHS[k] == 1:
            part = times_transposed(jnp.concatenate(halves, axis=1), jnp.concatenate(rights, axis=1))
        else:
            part = sum(
                times_transposed(halves[p], rights[p]) * sixj[coef_index[s, p]] for p in range(NP)
            )
        part = part.reshape(-1, 2, ROWS, SB)
        if k == FIRST:
            acc[s, zs] = part
        else:
            acc[s, zs] += part

    mine, theirs = here.xl, 1 - here.xl
    near, low = here.z // 4, here.z % 4
    flips = (low, low + 1 - 2 * (low % 2), (low + 2) % 4, 3 - low)
    places = [4 * near + flips[m] for m in range(4)]
    places += [4 * (1 - near) + flips[m] for m in range(4)]

    def partial_sum(m, whose):
        return jnp.concatenate([acc[s, places[m], whose] for s in range(2)], axis=0)

    def to_partner(m):
        return pltpu.make_async_remote_copy(
            src_ref=sa.at[m],
            dst_ref=ra.at[m],
            send_sem=rs_send.at[0],
            recv_sem=rs_recv.at[m],
            device_id=here.neighbour(XP),
            device_id_type=MESH,
        )

    def along_z(m):
        return pltpu.make_async_remote_copy(
            src_ref=sb.at[m],
            dst_ref=out.at[m],
            send_sem=rs_send.at[1],
            recv_sem=rs_recv.at[8 + m],
            device_id=here.at(z=places[m]),
            device_id_type=MESH,
        )

    def share(m):
        sa[m] = partial_sum(m, theirs).astype(jnp.bfloat16)
        to_partner(m).start()

    def last_tasks(k):
        tasks = []
        for z, count, ms in (
            (4 * (1 - near), 4, (4, 5, 6, 7)),
            (4 * near, 4, (3, 2, 1, 0)),
        ):
            n = SB // 8
            rows = pl.ds(pl.multiple_of(z * n, 2 * n), count * n)
            zs = pl.ds(z, count)
            for s in range(2):
                tasks += [functools.partial(first, k, p, s, rows) for p in range(NP)]
                tasks.append(functools.partial(second, k, s, rows, zs))
            tasks += [functools.partial(share, m) for m in ms]
        return tasks

    todo = []
    loaded = set()
    for k, what in ORDER:
        if k == READY:
            if what == FIRST:
                for load in (load_left, load_right, *tables):
                    load.wait()
            for i in range(len(MESSAGES[what])):
                arrival(what, i)
            if what == LAST:
                todo += last_tasks(what)
            else:
                for s in range(2):
                    todo += [functools.partial(first, what, p, s) for p in range(NP)]
                    todo.append(functools.partial(second, what, s))
        elif k == WORK:
            for task in todo[:what]:
                task()
            todo = todo[what:]
        else:
            if k not in loaded:
                loaded.add(k)
                loads[k].wait()
                if len(loaded) == NCH:
                    for load in (load_left, load_right, *tables):
                        load.start()
            for i in MESSAGES[k][what][5]:
                arrival(k, i)
            message(k, what).start()

    for task in todo:
        task()

    for m in (4, 5, 6, 7, 3, 2, 1):
        to_partner(m).wait_recv()
        sb[m] = (partial_sum(m, mine) + ra[m].astype(jnp.float32)).astype(jnp.bfloat16)
        along_z(m).start()
    to_partner(0).wait_recv()
    sb[0] = (partial_sum(0, mine) + ra[0].astype(jnp.float32)).astype(jnp.bfloat16)
    keep = pltpu.make_async_copy(sb.at[0], out.at[0], rs_recv.at[8])
    keep.start()
    for m in (4, 5, 6, 7, 3, 2, 1):
        along_z(m).wait_recv()
    keep.wait()

    rb = sb.at[pl.ds(0, 7)]
    for k in range(NCH):
        rows = sum((hi - lo) * (2 if sector == BOTH else 1) for _, _, lo, hi, sector, _ in MESSAGES[k])
        assert rows % SB == 0
        ref = gs[k].at[pl.ds(0, rows // SB)]
        pltpu.make_async_copy(ref, ref, send_sem.at[k]).wait()
    pltpu.make_async_copy(sa, sa, rs_send.at[0]).wait()
    pltpu.make_async_copy(rb, rb, rs_send.at[1]).wait()


def on_device(psi, left_ops, right_ops, source, coef_index, sixj):
    hbm = pl.BlockSpec(memory_space=pltpu.HBM)
    bf16, f32 = jnp.bfloat16, jnp.float32
    parts = pl.pallas_call(
        kernel,
        name="sigma",
        out_shape=jax.ShapeDtypeStruct((8, 2 * ROWS, SB), bf16),
        in_specs=[hbm] * 6,
        out_specs=pl.BlockSpec(memory_space=pl.ANY),
        scratch_shapes=[
            [pltpu.VMEM((32, SB, 128 * w), bf16) for w in WIDTHS],
            pltpu.SMEM((2, NP), jnp.int32),
            pltpu.SMEM((2, NP), jnp.int32),
            pltpu.SMEM((64,), f32),
            pltpu.VMEM((NP, 2, SB, SB), bf16),
            pltpu.VMEM((NP, 2, SB, SB), bf16),
            pltpu.VMEM((2, NP, SB, 128 * max(WIDTHS)), bf16),
            pltpu.VMEM((2, 8, 2, ROWS, SB), f32),
            pltpu.VMEM((8, 2 * ROWS, SB), bf16),
            pltpu.VMEM((8, 2 * ROWS, SB), bf16),
            pltpu.VMEM((8, 2 * ROWS, SB), bf16),
            pltpu.SemaphoreType.DMA((NCH + 5,)),
            pltpu.SemaphoreType.DMA((NCH,)),
            pltpu.SemaphoreType.DMA((NCH, max(len(table) for table in MESSAGES))),
            pltpu.SemaphoreType.DMA((2,)),
            pltpu.SemaphoreType.DMA((16,)),
        ],
        compiler_params=pltpu.CompilerParams(
            collective_id=0, has_side_effects=True, vmem_limit_bytes=56 * 2**20
        ),
    )(psi, left_ops, right_ops, source.T, coef_index.T, sixj)
    mine = jnp.sum(parts.astype(f32), axis=0).astype(bf16)
    return jnp.transpose(mine.reshape(2, ROWS, SB), (1, 0, 2))


def solution(mesh):
    placed = (
        P("sec", None, None),
        P("opg", "sec", None, None),
        P("opg", "sec", None, None),
        P("opg", "sec"),
        P("opg", "sec"),
        P(),
    )
    return jax.shard_map(
        on_device, mesh=mesh, in_specs=placed, out_specs=P("opg", "sec", None), check_vma=False
    )
```
